32 devices in a mesh: groups: 2 (over y), tier: 4 (over z), dir: 2 (over x), sub: 2 (over core).
Axes of the slice: x: 2, y: 2, z: 4, core: 2. Of those that a mesh axis runs over, the one named last changes fastest.
Arguments:
- auxiliary: float32 [1024, 4608], P(('groups', 'tier', 'sub')), parts along dimension 0, may hold values from -6 to 6
- hamiltonian: float32 [96, 48], P('groups'), parts along dimension 0, may hold values from -0.875 to 0.875
- coupling_re: float32 [192], P('groups'), parts along dimension 0, may hold values from 0.25 to 2
- coupling_im: float32 [192], P('groups'), parts along dimension 0, may hold values from -1 to 1
- damping_rates: float32 [192], P('groups'), parts along dimension 0, may hold values from 0.05 to 0.5
- routes: int32 [1024, 4], P(('groups', 'tier', 'sub')), parts along dimension 0, may hold values from 0 to 15, all different within a row; in each aligned block of 64 rows (0 to 63, 64 to 127, ...) at most 32 rows name the same one
- partner: int32 [1024, 4], P(('groups', 'tier', 'sub')), parts along dimension 0, may hold values from 0 to 63
- within: int32 [1024, 4], P(('groups', 'tier', 'sub')), parts along dimension 0, may hold values from 0 to 47
- levels: int32 [1024, 4], P(('groups', 'tier', 'sub')), parts along dimension 0, may hold values from 1 to 4
Outputs:
- slope_first: float32 [1024, 4608], P(('groups', 'tier', 'sub')), parts along dimension 0
- slope_second: float32 [1024, 4608], P(('groups', 'tier', 'sub')), parts along dimension 0
The draws below stay inside these ranges and needn't reach their ends.
There are 2 independent parts, one for each index of `groups`. The reference program is written for one: setup_inputs(seed, part) draws one part's arguments, and reference() takes and returns one part's arrays. A program takes and returns all parts, laid end to end along the dimension named above; each array names one. Nothing has to cross between parts.
Inputs may be any that keep to these rules, and one draw needn't show every extreme that they name: `routes`: within the rows of one group (64 matrices in a row) no route number appears more than 32 times, and the 4 numbers of one matrix differ.
All inputs are finite; a program needn't handle non-finite values.
Results may differ from the reference program's by a relative error of at most 0.00005.
Values sent between devices are 32-bit elements; how exact they have to be, the bound alone decides.
A program may use at most 128 MiB of HBM per device.

```python
import math
import jax
import jax.numpy as jnp
import numpy as np
from jax import lax

NPIG = 48
K = 96
KD = 48
LINKS = 4
MAT_DEV = 64
MAT = 512
NN = 4608
CAP = 32
N_TIER = 4
N_DIR = 2
N_SUB = 2


def plant(values, own_key, least, high):
    shape = values.shape
    spot = [jax.random.randint(jax.random.fold_in(own_key, axis), (), 0, shape[axis]) for axis in range(len(shape))]
    values = values.at[tuple(spot)].set(least)
    longest = shape.index(max(shape))
    spot[longest] = (spot[longest] + 1) % shape[longest]
    return values.at[tuple(spot)].set(high)


def block_levels(key, dims, split, smallest, top_value):
    loudness, own = 1.0, jax.random.fold_in(key, 6)
    for dim, parts in split:
        draws = jnp.exp(jax.random.uniform(jax.random.fold_in(own, dim), (parts,), jnp.float32, smallest / len(split), top_value / len(split)))
        loudness = loudness * jnp.repeat(draws, dims[dim] // parts).reshape([-1 if axis == dim else 1 for axis in range(len(dims))])
    return loudness


def deal_out(rng, own, number, rows, amount, top, most, skew):
    order = jax.random.permutation(rng, amount)
    crowded, usual = shares(amount, rows * top, most, skew, True), shares(amount, rows * top, most, skew, False)
    places = jnp.arange(amount)

    def named(tallies, offset_by):
        used = int((tallies > 0).sum())
        fixed = max(1, used // 4)
        passed = fixed + (places - fixed + offset_by * (used - fixed)) % max(1, amount - fixed)
        return jnp.zeros((amount,), jnp.int32).at[order[jnp.where(places < fixed, places, passed)]].set(jnp.asarray(tallies, jnp.int32))

    tallies = jnp.where(number % 4 == 0, named(crowded, number // 4), named(usual, number - number // 4 - 1))
    mixed = jax.random.permutation(jax.random.fold_in(own, 3), amount)
    donor, taker = mixed[0:amount // 2 * 2:2], mixed[1:amount // 2 * 2:2]
    slack = jnp.minimum(tallies[donor] - 1, most - tallies[taker]) // 2
    slack = jnp.where((donor == order[0]) | (taker == order[0]) | (tallies[taker] == 0), 0, jnp.maximum(slack, 0))
    passed = jax.random.randint(jax.random.fold_in(own, 4), (amount // 2,), 0, 1 << 20) % (slack + 1)
    tallies = tallies.at[donor].add(-passed).at[taker].add(passed)
    members = jnp.searchsorted(jnp.cumsum(tallies), jnp.arange(rows * top), side="right").astype(jnp.int32)
    grid = members.reshape(top, rows).T
    grid = grid[jax.random.permutation(jax.random.fold_in(own, 1), rows)]
    offset_by = jax.random.randint(jax.random.fold_in(own, 2), (rows, 1), 0, top)
    return jnp.take_along_axis(grid, (jnp.arange(top)[None, :] + offset_by) % top, axis=1)


def shares(count, total, reach, slope, full):
    weights = [(1 << 20) // math.isqrt(rank ** slope) + 1 for rank in range(1, count + 1)]
    largest = reach if full else min(reach, max(-(-total // count), total * weights[0] // sum(weights)))
    least = 1 if total - largest >= count - 1 else 0
    given, spare = [largest] + [least] * (count - 1), total - largest - least * (count - 1)
    while spare > 0:
        free = [i for i in range(1, count) if given[i] < largest] or [i for i in range(1, count) if given[i] < reach]
        whole, budget = sum([weights[i] for i in free]), spare
        for i in free:
            addition = min(reach - given[i], max(1, budget * weights[i] // whole), spare)
            given[i] = given[i] + addition
            spare = spare - addition
    return np.array(given)


def scatter_about(own_key, dims, width, bound, pieces=(), kind=jnp.bfloat16):
    factor_of = block_levels(own_key, dims, pieces, -0.22, 0.18) if pieces else 1.0
    drawn = jax.random.normal(own_key, dims, jnp.float32) * width * factor_of
    return jnp.minimum(jnp.maximum(drawn, -bound), bound).astype(kind)


def setup_inputs(seed: int = 0, part: int = 0) -> dict:
    key_list = jax.random.split(jax.random.key(seed), 10)
    part_splits = jax.random.split(jax.random.fold_in(key_list[9], part), 10)
    auxiliary = scatter_about(part_splits[0], (MAT, NN), 1.0, 6.0, ((0, 8),), jnp.float32)
    hamiltonian = scatter_about(part_splits[1], (NPIG, NPIG), NPIG ** -0.5, 0.875, (), jnp.float32)
    coupling_re = jnp.clip(jnp.exp(jax.random.uniform(part_splits[2], (K,), jnp.float32, math.log(0.25), math.log(2.0))), 0.25, 2.0)
    coupling_im = jnp.clip(jax.random.uniform(part_splits[3], (K,), jnp.float32, -1.0, 1.0), -1.0, 1.0)
    damping_rates = jnp.clip(jnp.exp(jax.random.uniform(part_splits[4], (K,), jnp.float32, math.log(0.05), math.log(0.5))), 0.05, 0.5)
    routes_keys = jax.random.split(jax.random.fold_in(part_splits[5], 1), MAT // MAT_DEV)
    routes_turns = jax.random.permutation(jax.random.fold_in(part_splits[5], 3), MAT // MAT_DEV)
    routes = jax.vmap(lambda own, number: deal_out(jax.random.fold_in(part_splits[5], 2), own, number, MAT_DEV, N_TIER * N_SUB * N_DIR, LINKS, CAP, 2))(routes_keys, routes_turns).reshape((MAT, LINKS))
    partner = plant(jax.random.randint(part_splits[6], (MAT, LINKS), 0, MAT_DEV), jax.random.fold_in(part_splits[6], 1), 0, MAT_DEV - 1).astype(jnp.int32)
    within = plant(jax.random.randint(part_splits[7], (MAT, LINKS), 0, KD), jax.random.fold_in(part_splits[7], 1), 0, KD - 1).astype(jnp.int32)
    levels = plant(jax.random.randint(part_splits[8], (MAT, LINKS), 1, 5), jax.random.fold_in(part_splits[8], 1), 1, 4).astype(jnp.int32)
    return {"auxiliary": auxiliary, "hamiltonian": hamiltonian, "coupling_re": coupling_re, "coupling_im": coupling_im, "damping_rates": damping_rates, "routes": routes, "partner": partner, "within": within, "levels": levels}


precise = lax.Precision.HIGHEST
step_length = 0.2

def derivative(stacked, hamiltonian, child_index, parent_index, pigment, up_scale, scaled_real, scaled_imag, decay_rate):
    matrix_total = stacked.shape[0]
    dimension = hamiltonian.shape[0]
    blocked = stacked.reshape(matrix_total, 2, dimension, dimension)
    symmetric = 0.5 * (hamiltonian + hamiltonian.T)
    difference = jnp.einsum('ij,gcjk->gcik', symmetric, blocked, precision=precise) - jnp.einsum('gcij,jk->gcik', blocked, symmetric, precision=precise)
    result = jnp.stack([difference[:, 1], -difference[:, 0]], axis=1) - decay_rate[:, None, None, None] * blocked
    child_rows = blocked[child_index, :, pigment, :] * up_scale[:, None, None]
    child_cols = blocked[child_index, :, :, pigment] * up_scale[:, None, None]
    parent_rows = blocked[parent_index, :, pigment, :]
    parent_cols = blocked[parent_index, :, :, pigment]
    up_rows = jnp.stack([child_rows[:, 1], -child_rows[:, 0]], axis=1)
    up_cols = jnp.stack([-child_cols[:, 1], child_cols[:, 0]], axis=1)
    real_part = scaled_real[:, None]
    imag_part = scaled_imag[:, None]
    down_rows = jnp.stack([real_part * parent_rows[:, 1] + imag_part * parent_rows[:, 0], -real_part * parent_rows[:, 0] + imag_part * parent_rows[:, 1]], axis=1)
    down_cols = jnp.stack([-real_part * parent_cols[:, 1] + imag_part * parent_cols[:, 0], real_part * parent_cols[:, 0] + imag_part * parent_cols[:, 1]], axis=1)
    targets = jnp.concatenate([parent_index, child_index]) * dimension + jnp.concatenate([pigment, pigment])
    row_sums = jax.ops.segment_sum(jnp.concatenate([up_rows, down_rows]), targets, num_segments=matrix_total * dimension)
    col_sums = jax.ops.segment_sum(jnp.concatenate([up_cols, down_cols]), targets, num_segments=matrix_total * dimension)
    row_dense = row_sums.reshape(matrix_total, dimension, 2, dimension).transpose(0, 2, 1, 3)
    col_dense = col_sums.reshape(matrix_total, dimension, 2, dimension).transpose(0, 2, 3, 1)
    return (result + row_dense + col_dense).reshape(matrix_total, -1)

def reference(auxiliary, hamiltonian, coupling_re, coupling_im, damping_rates, routes, partner, within, levels):
    matrix_total = auxiliary.shape[0]
    link_count = routes.shape[1]
    child_index = jnp.repeat(jnp.arange(matrix_total, dtype=jnp.int32), link_count)
    route_flat = routes.reshape(-1)
    parent_index = route_flat // N_DIR * MAT_DEV + partner.reshape(-1)
    direction = route_flat % N_DIR * KD + within.reshape(-1)
    pigment = direction // 2
    occupation = levels.reshape(-1).astype(jnp.float32)
    coupling_real = coupling_re[direction]
    coupling_imag = coupling_im[direction]
    magnitude = jnp.sqrt(coupling_real * coupling_real + coupling_imag * coupling_imag)
    up_scale = jnp.sqrt(occupation * magnitude)
    down_scale = jnp.sqrt(occupation / magnitude)
    decay_rate = lax.optimization_barrier(jnp.sum((occupation * damping_rates[direction]).reshape(matrix_total, link_count), axis=1))
    slope_first = derivative(auxiliary, hamiltonian, child_index, parent_index, pigment, up_scale, down_scale * coupling_real, down_scale * coupling_imag, decay_rate)
    midpoint = auxiliary + 0.5 * step_length * slope_first
    slope_second = derivative(midpoint, hamiltonian, child_index, parent_index, pigment, up_scale, down_scale * coupling_real, down_scale * coupling_imag, decay_rate)
    return (slope_first, slope_second)
```

```python
import functools

import jax
import jax.numpy as jnp
from jax import lax
from jax.experimental import pallas as pl
from jax.experimental.pallas import tpu as pltpu
from jax.sharding import PartitionSpec as P

precise = lax.Precision.HIGHEST
step_length = 0.2
LANES = 128
F32 = jnp.float32
BF16 = jnp.bfloat16
MESH = pl.DeviceIdType.MESH


def iota(shape, axis):
    return lax.broadcasted_iota(jnp.int32, shape, axis)


def split(values):
    high = values.astype(BF16)
    return high, (values - high.astype(F32)).astype(BF16)


def mm(a, b):
    return jnp.dot(a, b, preferred_element_type=F32)


def exact(a, b):
    return jnp.dot(a, b, preferred_element_type=F32, precision=precise)


def swapped(strips, dim):
    lane = iota(strips.shape, 1)
    down = pltpu.roll(strips, LANES - dim, 1)
    up = pltpu.roll(strips, dim, 1)
    return jnp.where(lane < dim, down, jnp.where(lane < 2 * dim, -up, 0.0))


def turn(block, dim):
    flipped = block.T
    pad = jnp.zeros((dim, LANES - 2 * dim), F32)
    return jnp.concatenate([flipped[:dim], flipped[dim : 2 * dim], pad], axis=1)


def kernel(
    shapes, aux, weight, cols, rows, table, first, second,
    mid, dense, t_hi, t_lo, take, put, keys_out, keys_in, own_keys, sizes,
    outbox, inbox, v_hi, v_lo, rate,
    key_send, key_recv, out_send, out_recv, fwd_send, fwd_recv,
):
    count, dim, links, n, n_sub, capacity = shapes
    total = count * dim
    block = 2 * capacity
    width = 256 if n * block >= 256 else n * block
    per = width // block
    n_sets = n // per
    tall = 8 * dim

    me = lax.axis_index("tier") * n_sub + lax.axis_index("sub")
    part = lax.rem(lax.axis_index("dir"), 2)
    other = lax.axis_index("dir") + 1 - 2 * part

    def place(peer):
        return {"tier": peer // n_sub, "sub": lax.rem(peer, n_sub)}

    def peer_of(step):
        return lax.rem(me + step, n)

    barrier = pltpu.get_barrier_semaphore()

    @pl.loop(1, n)
    def _(step):
        pl.semaphore_signal(barrier, inc=1, device_id=place(peer_of(step)), device_id_type=MESH)

    pl.semaphore_signal(barrier, inc=1, device_id={"dir": other}, device_id_type=MESH)
    pl.semaphore_wait(barrier, n)

    route_col = cols[:, 0:1]
    route_row = rows[0:1, :]
    alike = route_col == route_row
    earlier = iota((links, links), 1) < iota((links, links), 0)
    later = iota((links, links), 0) < iota((links, links), 1)
    rank_col = jnp.sum(jnp.where(alike & earlier, 1.0, 0.0), axis=1, keepdims=True)
    rank_row = jnp.sum(jnp.where(alike & later, 1.0, 0.0), axis=0, keepdims=True)
    slot_col = (route_col + rank_col).astype(jnp.int32)
    slot_row = (route_row + rank_row).astype(jnp.int32)
    row_attr = rows[...]

    @pl.loop(0, n)
    def _(q):
        lane = iota((links, width), 1)
        within = slot_col - q * capacity
        inside = (within >= 0) & (within < capacity)
        mine = jnp.where((within + lax.rem(me, per) * block == lane) & inside, 1.0, 0.0)
        keys_out[q] = exact(row_attr, mine)
        kept = jnp.where((within + lax.rem(q, per) * block + capacity == lane) & inside, 1.0, 0.0)
        own_keys[q] = exact(row_attr, kept)

    def key_copy(peer, index):
        return pltpu.make_async_remote_copy(
            src_ref=keys_out.at[peer],
            dst_ref=keys_in.at[index],
            send_sem=key_send.at[peer],
            recv_sem=key_recv.at[index],
            device_id=place(peer),
            device_id_type=MESH,
        )

    @pl.loop(1, n)
    def _(step):
        key_copy(peer_of(step), me).start()

    keys_in[me] = keys_out[me]

    level = cols[:, 3:4]
    chosen = jnp.where(cols[:, 4:5].astype(jnp.int32) == iota((links, table.shape[0]), 1), 1.0, 0.0)
    found = exact(chosen, table[...])
    found = found * jnp.where(iota((links, LANES), 1) < 3, jnp.sqrt(level), level)
    owner = jnp.where(iota((count, links), 1) // (links // count) == iota((count, links), 0), 1.0, 0.0)
    rate[...] = exact(owner, found)

    @pl.loop(0, n_sets)
    def _(g):
        row = iota((width, links), 0)
        wanted = (g * per + row // block) * capacity + lax.rem(row, capacity)
        placed = jnp.where(wanted == slot_row, 1.0, 0.0)
        sizes[g] = exact(placed, found)

    def build(source):
        for m in range(dim):
            real = source[:, m * dim : (m + 1) * dim]
            imag = source[:, (dim + m) * dim : (dim + m + 1) * dim]
            pad = jnp.zeros((count, LANES - 2 * dim), F32)
            dense[pl.ds(m, count, stride=dim), :] = jnp.concatenate([real, imag, pad], axis=1)

        @pl.loop(0, count // 8)
        def _(chunk):
            for k in range(8):
                at = pl.ds(pl.multiple_of(chunk * tall + k * dim, 16), dim)
                straight = dense[at, :]
                t_hi[0, at, :], t_lo[0, at, :] = split(straight)
                t_hi[1, at, :], t_lo[1, at, :] = split(turn(straight, dim))

    build(aux)
    weight_hi, weight_lo = split(weight[...])

    @pl.loop(1, n)
    def _(step):
        key_copy(me, peer_of(step)).wait_recv()

    @pl.loop(0, n_sets)
    def _(g):
        key = jnp.zeros((8, width), F32)
        for k in range(per):
            at = g * per + k
            key = key + jnp.broadcast_to(keys_in[at][1:2], (8, width))
            key = key + jnp.broadcast_to(own_keys[at][2:3], (8, width))
        as_row = key[0:1].astype(jnp.int32) - 1
        as_col = key.T[:, 0:1].astype(jnp.int32) - 1

        @pl.loop(0, total // tall)
        def _(chunk):
            at = pl.multiple_of(chunk * tall, LANES)
            below = iota((tall, width), 0) + at
            put[g, pl.ds(at, tall), :] = jnp.where(below == as_row, 1.0, 0.0).astype(BF16)
            across = iota((width, tall), 1) + at
            take[g, :, pl.ds(at, tall)] = jnp.where(across == as_col, 1.0, 0.0).astype(BF16)

    @pl.loop(1, n)
    def _(step):
        key_copy(peer_of(step), me).wait_send()

    sign = (1 - 2 * part).astype(F32)

    def out_copy(turn_no, peer, index):
        return pltpu.make_async_remote_copy(
            src_ref=outbox.at[turn_no, peer],
            dst_ref=inbox.at[turn_no, part, index],
            send_sem=out_send.at[turn_no, peer],
            recv_sem=out_recv.at[turn_no, index],
            device_id=place(peer),
            device_id_type=MESH,
        )

    def forward(turn_no, index, which):
        return pltpu.make_async_remote_copy(
            src_ref=inbox.at[turn_no, which, index],
            dst_ref=inbox.at[turn_no, which, index],
            send_sem=fwd_send.at[turn_no, index],
            recv_sem=fwd_recv.at[turn_no, index],
            device_id={"dir": other},
            device_id_type=MESH,
        )

    def section(turn_no, source, target):
        @pl.loop(0, n_sets)
        def _(g):
            one_hot = take[g]
            strips = mm(one_hot, t_hi[part]) + mm(one_hot, t_lo[part])
            upper = (sign * sizes[g][:, 0:1]) * swapped(strips, dim)
            for k in range(per):
                at = g * per + k
                outbox[turn_no, at, 0:capacity] = upper[k * block + capacity : (k + 1) * block]
                outbox[turn_no, at, capacity:block] = strips[k * block : k * block + capacity]

                @pl.when(at != me)
                def _():
                    out_copy(turn_no, at, me).start()

        inbox[turn_no, part, me] = outbox[turn_no, me]
        forward(turn_no, me, part).start()

        @pl.loop(1, n)
        def _(step):
            peer = peer_of(step)
            out_copy(turn_no, me, peer).wait_recv()
            forward(turn_no, peer, part).start()

        @pl.loop(0, n)
        def _(q):
            forward(turn_no, q, 1 - part).wait_recv()

        @pl.loop(0, n_sets)
        def _(g):
            size = sizes[g]
            below = lax.rem(iota((width, LANES), 0), block) >= capacity
            for side in range(2):
                got = jnp.concatenate([inbox[turn_no, side, g * per + k] for k in range(per)], axis=0)
                lower = (1 - 2 * side) * size[:, 1:2] * swapped(got, dim) + size[:, 2:3] * got
                high, low = split(jnp.where(below, lower, got))
                v_hi[g, :, side * LANES : (side + 1) * LANES] = high
                v_lo[g, :, side * LANES : (side + 1) * LANES] = low

        @pl.loop(0, count // 8)
        def _(chunk):
            at = pl.ds(pl.multiple_of(chunk * tall, LANES), tall)
            spread = jnp.zeros((tall, 2 * LANES), F32)
            for g in range(n_sets):
                one_hot = put[g, at, :]
                spread = spread + mm(one_hot, v_hi[g]) + mm(one_hot, v_lo[g])
            own = []
            for side in range(2):
                high, low = t_hi[side, at, :], t_lo[side, at, :]
                own.append(mm(high, weight_hi) + mm(low, weight_hi) + mm(high, weight_lo))
            straight = spread[:, :LANES] + own[0]
            crossed = spread[:, LANES:] - own[1]
            for k in range(8):
                turned = turn(crossed[k * dim : (k + 1) * dim], dim)
                to = pl.ds(pl.multiple_of(chunk * tall + k * dim, 16), dim)
                dense[to, :] = straight[k * dim : (k + 1) * dim] + turned

        for c in range(dim // 8):
            picked = [dense[pl.ds(c * 8 + k, count, stride=dim), :] for k in range(8)]
            for half in range(2):
                at = slice((half * dim + c * 8) * dim, (half * dim + c * 8 + 8) * dim)
                flat = jnp.concatenate([p[:, half * dim : (half + 1) * dim] for p in picked], axis=1)
                target[:, at] = flat - rate[:, 3:4] * source[:, at]

        @pl.loop(1, n)
        def _(step):
            out_copy(turn_no, peer_of(step), me).wait_send()

        @pl.loop(0, n)
        def _(q):
            forward(turn_no, q, part).wait_send()

    section(0, aux, first)
    mid[...] = aux[...] + (0.5 * step_length) * first[...]
    build(mid)
    section(1, mid, second)


def per_device(
    auxiliary, hamiltonian, coupling_re, coupling_im, damping_rates, routes, partner, within, levels
):
    count, entries = auxiliary.shape
    dim = hamiltonian.shape[0]
    direction_count = coupling_re.shape[0]
    per_row = routes.shape[1]
    links = count * per_row
    n = lax.axis_size(("tier", "sub"))
    blocks = lax.axis_size("dir")
    per_block = direction_count // blocks
    each = max(2, 2 * links // (n * blocks))
    capacity = each * blocks
    block = 2 * capacity
    width = min(256, n * block)
    n_sets = n * block // width

    direction = (routes % blocks) * per_block + within
    pigment = direction // 2
    child = jnp.arange(count, dtype=jnp.int32)[:, None] * dim + pigment
    attributes = jnp.stack(
        [routes * each, partner * dim + pigment + 1, child + 1, levels, direction] + [levels] * 3, axis=-1
    )
    attributes = attributes.reshape(links, 8).astype(F32)
    root = jnp.sqrt(jnp.sqrt(coupling_re * coupling_re + coupling_im * coupling_im))
    table = jnp.stack([root, coupling_re / root, coupling_im / root, damping_rates], axis=1)
    table = jnp.pad(table, ((0, 0), (0, LANES - 4)))
    symmetric = 0.5 * (hamiltonian + hamiltonian.T)
    zero = jnp.zeros_like(symmetric)
    weight = jnp.concatenate(
        [jnp.concatenate([zero, symmetric], axis=1), jnp.concatenate([-symmetric, zero], axis=1)], axis=0
    )
    weight = jnp.pad(weight, ((0, LANES - 2 * dim), (0, LANES - 2 * dim)))

    total = count * dim
    shapes = (count, dim, links, n, lax.axis_size("sub"), capacity)
    vmem = pl.BlockSpec(memory_space=pltpu.VMEM)
    dma = pltpu.SemaphoreType.DMA
    out = jax.ShapeDtypeStruct((count, entries), F32)
    return pl.pallas_call(
        functools.partial(kernel, shapes),
        out_shape=(out, out),
        in_specs=[vmem] * 5,
        out_specs=(vmem, vmem),
        scratch_shapes=[
            pltpu.VMEM((count, entries), F32),
            pltpu.VMEM((total, LANES), F32),
            pltpu.VMEM((2, total, LANES), BF16),
            pltpu.VMEM((2, total, LANES), BF16),
            pltpu.VMEM((n_sets, width, total), BF16),
            pltpu.VMEM((n_sets, total, width), BF16),
            pltpu.VMEM((n, 8, width), F32),
            pltpu.VMEM((n, 8, width), F32),
            pltpu.VMEM((n, 8, width), F32),
            pltpu.VMEM((n_sets, width, LANES), F32),
            pltpu.VMEM((2, n, block, LANES), F32),
            pltpu.VMEM((2, 2, n, block, LANES), F32),
            pltpu.VMEM((n_sets, width, 2 * LANES), BF16),
            pltpu.VMEM((n_sets, width, 2 * LANES), BF16),
            pltpu.VMEM((count, LANES), F32),
            dma((n,)),
            dma((n,)),
            dma((2, n)),
            dma((2, n)),
            dma((2, n)),
            dma((2, n)),
        ],
        compiler_params=pltpu.CompilerParams(
            collective_id=0, has_side_effects=True, vmem_limit_bytes=56 * 1024 * 1024
        ),
        cost_estimate=pl.CostEstimate(
            flops=10**10, bytes_accessed=6 * count * entries * 4, transcendentals=0
        ),
    )(auxiliary, weight, attributes, attributes.T, table)


def solution(mesh):
    split_all = P(("groups", "tier", "sub"), None)
    in_specs = (
        split_all,
        P("groups", None),
        P("groups"),
        P("groups"),
        P("groups"),
        split_all,
        split_all,
        split_all,
        split_all,
    )
    return jax.shard_map(
        per_device, mesh=mesh, in_specs=in_specs, out_specs=(split_all, split_all), check_vma=False
    )
```

```python
import functools

import jax
import jax.numpy as jnp
from jax import lax
from jax.experimental import pallas as pl
from jax.experimental.pallas import tpu as pltpu
from jax.sharding import PartitionSpec as P

precise = lax.Precision.HIGHEST
step_length = 0.2
LANES = 128
F32 = jnp.float32
BF16 = jnp.bfloat16
MESH = pl.DeviceIdType.MESH


def iota(shape, axis):
    return lax.broadcasted_iota(jnp.int32, shape, axis)


def split(values):
    high = values.astype(BF16)
    return high, (values - high.astype(F32)).astype(BF16)


def mm(a, b):
    return jnp.dot(a, b, preferred_element_type=F32)


def exact(a, b):
    return jnp.dot(a, b, preferred_element_type=F32, precision=precise)


def swapped(strips, dim):
    lane = iota(strips.shape, 1)
    down = pltpu.roll(strips, LANES - dim, 1)
    up = pltpu.roll(strips, dim, 1)
    return jnp.where(lane < dim, down, jnp.where(lane < 2 * dim, -up, 0.0))


def turn(block, dim):
    flipped = block.T
    pad = jnp.zeros((dim, LANES - 2 * dim), F32)
    return jnp.concatenate([flipped[:dim], flipped[dim : 2 * dim], pad], axis=1)


def kernel(
    shapes, aux, hamiltonian, baths, links_in, first, second,
    mid, dense, own, t_hi, t_lo, take, put, keys_out, keys_in, own_keys, sizes,
    outbox, inbox, v_hi, v_lo, rate,
    key_send, key_recv, out_send, out_recv, fwd_send, fwd_recv,
):
    count, dim, links, n, n_sub, blocks, each = shapes
    capacity = each * blocks
    total = count * dim
    block = 2 * capacity
    width = 256 if n * block >= 256 else n * block
    per = width // block
    n_sets = n // per
    tall = 8 * dim
    packed = outbox.shape[2]
    third = LANES // 4

    me = lax.axis_index("tier") * n_sub + lax.axis_index("sub")
    part = lax.rem(lax.axis_index("dir"), 2)
    other = lax.axis_index("dir") + 1 - 2 * part

    def place(peer):
        return {"tier": peer // n_sub, "sub": lax.rem(peer, n_sub)}

    def peer_of(step):
        return lax.rem(me + step, n)

    barrier = pltpu.get_barrier_semaphore()

    @pl.loop(1, n)
    def _(step):
        pl.semaphore_signal(barrier, inc=1, device_id=place(peer_of(step)), device_id_type=MESH)

    pl.semaphore_signal(barrier, inc=1, device_id={"dir": other}, device_id_type=MESH)
    pl.semaphore_wait(barrier, n)

    per_row = links // count

    def row_of(which):
        at = which * per_row
        return jnp.concatenate([links_in[at + k : at + k + 1, :] for k in range(per_row)], axis=1)

    kinds = [row_of(which).astype(F32) for which in range(4)]
    columns = jnp.concatenate(kinds + kinds, axis=0).T
    route_row, route_col = kinds[0], columns[:, 0:1]
    alike = route_col == route_row
    earlier = iota((links, links), 1) < iota((links, links), 0)
    later = iota((links, links), 0) < iota((links, links), 1)
    rank_col = jnp.sum(jnp.where(alike & earlier, 1.0, 0.0), axis=1, keepdims=True)
    rank_row = jnp.sum(jnp.where(alike & later, 1.0, 0.0), axis=0, keepdims=True)
    slot_col = (route_col * each + rank_col).astype(jnp.int32)
    slot_row = (route_row * each + rank_row).astype(jnp.int32)
    bath_count = baths.shape[1]
    integers = columns.astype(jnp.int32)
    direction = (integers[:, 0:1] & (blocks - 1)) * (bath_count // blocks) + integers[:, 2:3]
    pigment = lax.shift_right_logical(direction, 1)
    parent_key = (integers[:, 1:2] * dim + pigment + 1).astype(F32)
    child_key = (lax.rem(iota((links, 1), 0), count) * dim + pigment + 1).astype(F32)

    @pl.loop(0, n)
    def _(q):
        lane = iota((links, width), 1)
        within = slot_col - q * capacity
        inside = (within >= 0) & (within < capacity)
        there = jnp.where(inside, within + lax.rem(me, per) * block, -1)
        here = jnp.where(inside, within + lax.rem(q, per) * block + capacity, -1)
        sent = jnp.sum(jnp.where(there == lane, parent_key, 0.0), axis=0, keepdims=True)
        kept = jnp.sum(jnp.where(here == lane, child_key, 0.0), axis=0, keepdims=True)
        keys_out[q] = jnp.broadcast_to(sent, (8, width))
        own_keys[q] = jnp.broadcast_to(kept, (8, width))

    def key_copy(peer, index):
        return pltpu.make_async_remote_copy(
            src_ref=keys_out.at[peer],
            dst_ref=keys_in.at[index],
            send_sem=key_send.at[peer],
            recv_sem=key_recv.at[index],
            device_id=place(peer),
            device_id_type=MESH,
        )

    @pl.loop(1, n)
    def _(step):
        key_copy(peer_of(step), me).start()

    keys_in[me] = keys_out[me]

    level = columns[:, 3:4]
    chosen = direction == iota((links, bath_count), 1)

    def pick(row):
        return jnp.sum(jnp.where(chosen, row, 0.0), axis=1, keepdims=True)

    real, imag = baths[0:1, :], baths[1:2, :]
    root = jnp.sqrt(jnp.sqrt(real * real + imag * imag))
    size_root = jnp.sqrt(level)
    scales = [size_root * pick(root), size_root * pick(real / root), size_root * pick(imag / root)]
    scales.append(level * pick(baths[2:3, :]))
    lane = iota((links, LANES), 1)
    found = jnp.zeros((links, LANES), F32)
    for which, scale in enumerate(scales):
        found = jnp.where(lane == which, scale, found)
    both = jnp.concatenate(split(found), axis=1)
    owner = jnp.where(lax.rem(iota((count, links), 1), count) == iota((count, links), 0), 1.0, 0.0)
    rates = mm(owner.astype(BF16), both)
    rate[...] = rates[:, :LANES] + rates[:, LANES:]

    @pl.loop(0, n_sets)
    def _(g):
        row = iota((width, 1), 0)
        wanted = (g * per + row // block) * capacity + lax.rem(row, capacity)
        placed = jnp.where(wanted == slot_row, 1.0, 0.0).astype(BF16)
        size = mm(placed, both)
        sizes[g] = size[:, :LANES] + size[:, LANES:]

    def build(source):
        for m in range(dim):
            real = source[:, m * dim : (m + 1) * dim]
            imag = source[:, (dim + m) * dim : (dim + m + 1) * dim]
            pad = jnp.zeros((count, LANES - 2 * dim), F32)
            dense[pl.ds(m, count, stride=dim), :] = jnp.concatenate([real, imag, pad], axis=1)

        @pl.loop(0, count // 8)
        def _(chunk):
            for k in range(8):
                at = pl.ds(pl.multiple_of(chunk * tall + k * dim, 16), dim)
                straight = dense[at, :]
                t_hi[0, at, :], t_lo[0, at, :] = split(straight)
                t_hi[1, at, :], t_lo[1, at, :] = split(turn(straight, dim))

    build(aux)
    symmetric = 0.5 * (hamiltonian[...] + hamiltonian[...].T)
    zero = jnp.zeros((dim, dim), F32)
    side_pad = jnp.zeros((dim, LANES - 2 * dim), F32)
    weight = jnp.concatenate(
        [
            jnp.concatenate([zero, symmetric, side_pad], axis=1),
            jnp.concatenate([-symmetric, zero, side_pad], axis=1),
            jnp.zeros((LANES - 2 * dim, LANES), F32),
        ],
        axis=0,
    )
    weight_hi, weight_lo = split(weight)

    @pl.loop(1, n)
    def _(step):
        key_copy(me, peer_of(step)).wait_recv()

    @pl.loop(0, n_sets)
    def _(g):
        key = jnp.zeros((8, width), F32)
        for k in range(per):
            at = g * per + k
            key = key + jnp.broadcast_to(keys_in[at][0:1], (8, width))
            key = key + jnp.broadcast_to(own_keys[at][0:1], (8, width))
        as_row = key[0:1].astype(jnp.int32) - 1
        as_col = key.T[:, 0:1].astype(jnp.int32) - 1

        @pl.loop(0, total // tall)
        def _(chunk):
            at = pl.multiple_of(chunk * tall, LANES)
            put[g, pl.ds(at, tall), :] = jnp.where(iota((tall, width), 0) == as_row - at, 1.0, 0.0).astype(BF16)
            take[g, :, pl.ds(at, tall)] = jnp.where(iota((width, tall), 1) == as_col - at, 1.0, 0.0).astype(BF16)

    @pl.loop(1, n)
    def _(step):
        key_copy(peer_of(step), me).wait_send()

    sign = (1 - 2 * part).astype(F32)

    def out_copy(turn_no, peer, index):
        return pltpu.make_async_remote_copy(
            src_ref=outbox.at[turn_no, peer],
            dst_ref=inbox.at[turn_no, part, index],
            send_sem=out_send.at[turn_no, peer],
            recv_sem=out_recv.at[turn_no, index],
            device_id=place(peer),
            device_id_type=MESH,
        )

    def forward(turn_no, index, which):
        return pltpu.make_async_remote_copy(
            src_ref=inbox.at[turn_no, which, index],
            dst_ref=inbox.at[turn_no, which, index],
            send_sem=fwd_send.at[turn_no, index],
            recv_sem=fwd_recv.at[turn_no, index],
            device_id={"dir": other},
            device_id_type=MESH,
        )

    def packing(message):
        if packed == block:
            return message
        lane = iota((packed, LANES), 1)
        last = message[packed:]
        moved = [pltpu.roll(last, LANES - third * (k + 1), 1) for k in range(3)]
        return jnp.where(lane < 3 * third, message[:packed], jnp.concatenate(moved, axis=0))

    def unpacking(message):
        if packed == block:
            return message
        quarter = block // 4
        lane = iota((quarter, LANES), 1)
        last = jnp.zeros((quarter, LANES), F32)
        for k in range(3):
            piece = pltpu.roll(message[k * quarter : (k + 1) * quarter], third * (k + 1), 1)
            last = jnp.where((lane >= k * third) & (lane < (k + 1) * third), piece, last)
        clean = jnp.where(iota((packed, LANES), 1) < 3 * third, message, 0.0)
        return jnp.concatenate([clean, last], axis=0)

    home = me // per

    def section(turn_no, source, target):
        @pl.loop(0, n_sets)
        def _(k):
            g = lax.rem(home + k, n_sets)
            one_hot = take[g]
            strips = mm(one_hot, t_hi[part]) + mm(one_hot, t_lo[part])
            upper = (sign * sizes[g][:, 0:1]) * swapped(strips, dim)
            for k in range(per):
                at = g * per + k
                outbox[turn_no, at] = packing(
                    jnp.concatenate(
                        [
                            upper[k * block + capacity : (k + 1) * block],
                            strips[k * block : k * block + capacity],
                        ],
                        axis=0,
                    )
                )

                @pl.when(at != me)
                def _():
                    out_copy(turn_no, at, me).start()

                @pl.when(at == me)
                def _():
                    inbox[turn_no, part, me] = outbox[turn_no, me]
                    forward(turn_no, me, part).start()

        @pl.loop(0, count // 8)
        def _(chunk):
            at = pl.ds(pl.multiple_of(chunk * tall, LANES), tall)
            for side in range(2):
                high, low = t_hi[side, at, :], t_lo[side, at, :]
                product = mm(high, weight_hi) + mm(low, weight_hi) + mm(high, weight_lo)
                own[at, side * LANES : (side + 1) * LANES] = -product if side else product

        def arrive(k):
            g = lax.rem(home + n_sets - k, n_sets)

            @pl.loop(0, per)
            def _(i):
                peer = g * per + i

                @pl.when(peer != me)
                def _():
                    out_copy(turn_no, me, peer).wait_recv()
                    forward(turn_no, peer, part).start()

        arrive(0)
        for k in range(n_sets):
            if k < n_sets - 1:
                arrive(k + 1)
            g = lax.rem(home + n_sets - k, n_sets)

            @pl.loop(0, per)
            def _(i):
                forward(turn_no, g * per + i, 1 - part).wait_recv()

            size = sizes[g]
            below = lax.rem(iota((width, LANES), 0), block) >= capacity
            for side in range(2):
                got = [unpacking(inbox[turn_no, side, g * per + i]) for i in range(per)]
                got = jnp.concatenate(got, axis=0)
                lower = (1 - 2 * side) * size[:, 1:2] * swapped(got, dim) + size[:, 2:3] * got
                high, low = split(jnp.where(below, lower, got))
                v_hi[:, side * LANES : (side + 1) * LANES] = high
                v_lo[:, side * LANES : (side + 1) * LANES] = low

            @pl.loop(0, count // 8)
            def _(chunk):
                at = pl.ds(pl.multiple_of(chunk * tall, LANES), tall)
                one_hot = put[g, at, :]
                value = own[at, :] + mm(one_hot, v_hi[...]) + mm(one_hot, v_lo[...])
                if k < n_sets - 1:
                    own[at, :] = value
                else:
                    for j in range(8):
                        rows = slice(j * dim, (j + 1) * dim)
                        to = pl.ds(pl.multiple_of(chunk * tall + j * dim, 16), dim)
                        dense[to, :] = value[rows, :LANES] + turn(value[rows, LANES:], dim)

        for c in range(dim // 8):
            picked = [dense[pl.ds(c * 8 + k, count, stride=dim), :] for k in range(8)]
            for half in range(2):
                at = slice((half * dim + c * 8) * dim, (half * dim + c * 8 + 8) * dim)
                flat = jnp.concatenate([p[:, half * dim : (half + 1) * dim] for p in picked], axis=1)
                target[:, at] = flat - rate[:, 3:4] * source[:, at]

        @pl.loop(1, n)
        def _(step):
            out_copy(turn_no, peer_of(step), me).wait_send()

        @pl.loop(0, n)
        def _(q):
            forward(turn_no, q, part).wait_send()

    section(0, aux, first)
    mid[...] = aux[...] + (0.5 * step_length) * first[...]
    build(mid)
    section(1, mid, second)


def per_device(
    auxiliary, hamiltonian, coupling_re, coupling_im, damping_rates, routes, partner, within, levels
):
    count, entries = auxiliary.shape
    dim = hamiltonian.shape[0]
    per_row = routes.shape[1]
    links = count * per_row
    n = lax.axis_size(("tier", "sub"))
    blocks = lax.axis_size("dir")
    each = max(2, 2 * links // (n * blocks))
    capacity = each * blocks
    block = 2 * capacity
    width = min(256, n * block)
    n_sets = n * block // width
    packed = block * 3 // 4 if block % 32 == 0 and 2 * dim == LANES * 3 // 4 else block

    links_in = jnp.concatenate([routes.T, partner.T, within.T, levels.T], axis=0)
    baths = jnp.stack([coupling_re, coupling_im, damping_rates])

    total = count * dim
    shapes = (count, dim, links, n, lax.axis_size("sub"), blocks, each)
    vmem = pl.BlockSpec(memory_space=pltpu.VMEM)
    dma = pltpu.SemaphoreType.DMA
    out = jax.ShapeDtypeStruct((count, entries), F32)
    return pl.pallas_call(
        functools.partial(kernel, shapes),
        out_shape=(out, out),
        in_specs=[vmem] * 4,
        out_specs=(vmem, vmem),
        scratch_shapes=[
            pltpu.VMEM((count, entries), F32),
            pltpu.VMEM((total, LANES), F32),
            pltpu.VMEM((total, 2 * LANES), F32),
            pltpu.VMEM((2, total, LANES), BF16),
            pltpu.VMEM((2, total, LANES), BF16),
            pltpu.VMEM((n_sets, width, total), BF16),
            pltpu.VMEM((n_sets, total, width), BF16),
            pltpu.VMEM((n, 8, width), F32),
            pltpu.VMEM((n, 8, width), F32),
            pltpu.VMEM((n, 8, width), F32),
            pltpu.VMEM((n_sets, width, LANES), F32),
            pltpu.VMEM((2, n, packed, LANES), F32),
            pltpu.VMEM((2, 2, n, packed, LANES), F32),
            pltpu.VMEM((width, 2 * LANES), BF16),
            pltpu.VMEM((width, 2 * LANES), BF16),
            pltpu.VMEM((count, LANES), F32),
            dma((n,)),
            dma((n,)),
            dma((2, n)),
            dma((2, n)),
            dma((2, n)),
            dma((2, n)),
        ],
        compiler_params=pltpu.CompilerParams(
            collective_id=0, has_side_effects=True, vmem_limit_bytes=56 * 1024 * 1024
        ),
        cost_estimate=pl.CostEstimate(
            flops=10**10, bytes_accessed=6 * count * entries * 4, transcendentals=0
        ),
    )(auxiliary, hamiltonian, baths, links_in)


def solution(mesh):
    split_all = P(("groups", "tier", "sub"), None)
    in_specs = (
        split_all,
        P("groups", None),
        P("groups"),
        P("groups"),
        P("groups"),
        split_all,
        split_all,
        split_all,
        split_all,
    )
    return jax.shard_map(
        per_device, mesh=mesh, in_specs=in_specs, out_specs=(split_all, split_all), check_vma=False
    )
```
